32 devices in a mesh: tm: 4 (over y, x), chan: 8 (over z, core).
Axes of the slice: x: 2, y: 2, z: 4, core: 2. Of those that a mesh axis runs over, the one named last changes fastest.
Arguments:
- voltages: bfloat16 [2, 128, 2048, 1024], P(None, 'tm', 'chan'), may hold values from -6 to 6
- subspace: float32 [8, 256, 32, 1024], P('chan', 'tm'), may hold values from -0.1875 to 0.1875
- order: int32 [256], replicated, may hold values from 0 to 255, each once
- beam_seeds: int32 [256], replicated, may hold values from 1 to 65520
- flagged: int32 [16], replicated, may hold values from 0 to 511
Outputs:
- beams: bfloat16 [2, 8, 256, 512, 128], P(None, None, 'tm', 'chan')
- tracked: float32 [8, 256, 32, 1024], P('chan', 'tm')
The draws below stay inside these ranges and needn't reach their ends.
Inputs may be any that keep to these rules, and one draw needn't show every extreme that they name: `order`: each of 0 to 255 once. `flagged`: station numbers; a station may occur more than once.
All inputs are finite; a program needn't handle non-finite values.
Results may differ from the reference program's by a relative error of at most 0.0084.
Values may be sent and summed in bfloat16 or wider, within the bound.
A program may use at most 256 MiB of HBM per device.

```python
import math
import jax
import jax.numpy as jnp
from jax import lax

STATIONS = 512
SIG = 1024
CH = 2048
BEAMS = 256
RANK = 32
FLAGS = 16
SUB = 2
TIME = 128
GROUPS = 8
GROUP_CH = 256


def plant(entries, rng, low, largest):
    extent = entries.shape
    place = [jax.random.randint(jax.random.fold_in(rng, axis), (), 0, extent[axis]) for axis in range(len(extent))]
    entries = entries.at[tuple(place)].set(low)
    longest = extent.index(max(extent))
    place[longest] = (place[longest] + 1) % extent[longest]
    return entries.at[tuple(place)].set(largest)


def block_levels(rng, extent, split, low, high):
    def one(position, parts):
        steps = jax.random.uniform(jax.random.fold_in(jax.random.fold_in(rng, 6), position), (parts,), jnp.float32, low / len(split), high / len(split))
        return jnp.repeat(jnp.exp(steps), extent[position] // parts).reshape((-1,) + (1,) * (len(extent) - position - 1))

    factor_of = one(*split[0])
    for cut in split[1:]:
        factor_of = factor_of * one(*cut)
    return factor_of


def centred(key, shape, scale, most, cuts=(), held_as=jnp.bfloat16):
    array = jax.random.normal(key, shape, jnp.float32) * scale
    if len(cuts) > 0:
        array = block_levels(key, shape, cuts, -0.22, 0.18) * array
    return jnp.clip(array, min=-most, max=most).astype(held_as)


def setup_inputs(seed: int = 0) -> dict:
    arg_keys = jax.random.split(jax.random.key(seed), 6)
    return {
        "voltages": centred(arg_keys[0], (SUB, TIME, CH, SIG), 1.0, 6.0, ((1, 4), (2, 8))),
        "subspace": centred(arg_keys[1], (GROUPS, GROUP_CH, RANK, SIG), SIG ** -0.5, 0.1875, ((0, 8), (1, 4)), jnp.float32),
        "order": jax.random.permutation(arg_keys[2], GROUP_CH).astype(jnp.int32),
        "beam_seeds": plant(jax.random.randint(arg_keys[3], (BEAMS,), 1, 65521), jax.random.fold_in(arg_keys[3], 1), 1, 65520).astype(jnp.int32),
        "flagged": plant(jax.random.randint(arg_keys[4], (FLAGS,), 0, STATIONS), jax.random.fold_in(arg_keys[4], 1), 0, STATIONS - 1).astype(jnp.int32),
    }


TWO_PI = 2.0 * math.pi
FULL_PRECISION = lax.Precision.HIGHEST

def beam_weights(beam_seeds, channels, stations, total_channels):
    station_no = jnp.arange(stations, dtype=jnp.int32) + 1
    delays = (station_no[:, None] * beam_seeds[None, :] % 65521).astype(jnp.float32) / 65521.0
    frequency = 1.0 + channels.astype(jnp.float32) / total_channels
    angles = delays[None, :, :] * (TWO_PI * frequency)[:, None, None]
    factor = 1.0 / math.sqrt(stations)
    cosine = jnp.cos(angles) * factor
    sine_part = jnp.sin(angles) * factor
    upper = jnp.concatenate([cosine, sine_part], axis=2)
    under = jnp.concatenate([-sine_part, cosine], axis=2)
    return jnp.concatenate([upper, under], axis=1).astype(jnp.bfloat16)

def rounded_value(values):
    narrow = lax.optimization_barrier(values.astype(jnp.bfloat16))
    return narrow.astype(jnp.float32)

def power_step(voltage_input, tracked, steering_weight):
    sample_count = voltage_input.shape[0]
    wide_product = voltage_input.astype(jnp.float32)
    steering_weight_wide = steering_weight.astype(jnp.float32)
    coarse_channel = rounded_value(tracked)
    projected_input = rounded_value(jnp.einsum('xbj,bqj->bxq', wide_product, coarse_channel, precision=FULL_PRECISION))
    beam_image = jnp.einsum('nwg,wny->ngy', projected_input, wide_product, precision=FULL_PRECISION) + sample_count * tracked
    gram = jnp.einsum('crs,cks->crk', beam_image, beam_image, precision=FULL_PRECISION)
    lower = jnp.linalg.cholesky(gram)
    tracked = jax.scipy.linalg.solve_triangular(lower, beam_image, lower=True)
    subspace_vectors = rounded_value(tracked)
    lengthwise_axis = rounded_value(jnp.einsum('xbj,bqj->bxq', wide_product, subspace_vectors, precision=FULL_PRECISION))
    mixing = rounded_value(jnp.einsum('crs,csb->crb', subspace_vectors, steering_weight_wide, precision=FULL_PRECISION))
    direct_output = jnp.einsum('edi,diy->dye', wide_product, steering_weight_wide, precision=FULL_PRECISION)
    beams = direct_output - jnp.einsum('ctr,crb->cbt', lengthwise_axis, mixing, precision=FULL_PRECISION)
    return (tracked, beams.astype(jnp.bfloat16))

def reference(voltages, subspace, order, beam_seeds, flagged):
    signals = voltages.shape[-1]
    stations = signals // 2
    per_group = order.shape[0]
    marks = jnp.any(flagged[:, None] == jnp.arange(stations, dtype=jnp.int32)[None, :], axis=0)
    keep = jnp.where(marks, 0.0, 1.0).astype(jnp.bfloat16)
    keep = jnp.concatenate([keep, keep])

    def group_work(group):
        start = (group * per_group).astype(jnp.int32)
        block = lax.dynamic_slice_in_dim(voltages, start, per_group, 2)
        block = jnp.take(block, order, axis=2) * keep
        channels = start + order.astype(jnp.int32)
        steering_weight = beam_weights(beam_seeds, channels, stations, CH)
        state = lax.dynamic_index_in_dim(subspace, group, 0, keepdims=False)
        results = []
        for part in range(SUB):
            state, formed = power_step(block[part], state, steering_weight)
            results.append(formed)
        return (jnp.stack(results), state)
    formed_all, states = lax.map(group_work, jnp.arange(GROUPS, dtype=jnp.int32))
    return (jnp.moveaxis(formed_all, 0, 1), states)
```

```python
import functools
import math

import jax
import jax.numpy as jnp
import numpy as np
from jax import lax
from jax.experimental import pallas as pl
from jax.experimental.pallas import tpu as pltpu
from jax.sharding import PartitionSpec as P

CH = 2048
CHUNKS = 4
BLOCK = 8
TILE = 16

TWO_PI = 2.0 * math.pi
NT = (((1,), (1,)), ((), ()))
TN = (((0,), (0,)), ((), ()))


def series(func, odd):
    fit = np.polynomial.chebyshev.Chebyshev.interpolate(
        lambda r: func(TWO_PI * r), 11 if odd else 10, domain=[-0.5, 0.5]
    )
    powers = fit.convert(kind=np.polynomial.Polynomial).coef
    return [float(value) for value in powers[1 if odd else 0 :: 2]]


COS = series(np.cos, False)
SIN = series(np.sin, True)


def evaluate(coefficients, square, factor):
    total = coefficients[-1] * factor
    for value in coefficients[-2::-1]:
        total = total * square + value * factor
    return total


def arrange_kernel(chunks, per, place_ref, volt_ref, turn_ref, keep_ref, *rest):
    outs, (held, sems) = rest[:chunks], rest[chunks:]
    part, block = pl.program_id(0), pl.program_id(1)
    blocks = pl.num_programs(1)
    step = part * blocks + block
    half = lax.rem(step, 2)
    times = volt_ref.shape[1]

    def drain(which):
        for row in range(TILE):
            pltpu.make_async_copy(
                held.at[which, row], outs[0].at[0, 0, 0], sems.at[which, row]
            ).wait()

    @pl.when(step >= 2)
    def _():
        drain(half)

    for start in range(0, times, TILE):
        rows = volt_ref[0, start : start + TILE].reshape(TILE * TILE, -1)
        turned = jnp.dot(turn_ref[...], rows, preferred_element_type=jnp.float32)
        turned = (turned * keep_ref[...]).astype(jnp.bfloat16)
        held[half, :, start : start + TILE, :] = turned.reshape(TILE, TILE, -1)
    for row in range(TILE):
        place = place_ref[block * TILE + row]
        slots = chunks * per
        owner, local = place // slots, lax.rem(place, slots)
        chunk, inner = local // per, lax.rem(local, per)
        for index in range(chunks):

            @pl.when(chunk == index)
            def _():
                pltpu.make_async_copy(
                    held.at[half, row], outs[index].at[owner, inner, part], sems.at[half, row]
                ).start()

    @pl.when(step == 2 * blocks - 1)
    def _():
        drain(1 - half)
        drain(half)


def arrange(voltages, place, keep, owners, slots):
    parts, times, channels, signals = voltages.shape
    per = slots // CHUNKS
    row = jnp.arange(TILE * TILE)
    turn = (row[None, :] == (row % TILE * TILE + row // TILE)[:, None]).astype(jnp.bfloat16)
    shape = jax.ShapeDtypeStruct((owners, per, parts, times, signals), jnp.bfloat16)
    return pl.pallas_call(
        functools.partial(arrange_kernel, CHUNKS, per),
        grid_spec=pltpu.PrefetchScalarGridSpec(
            num_scalar_prefetch=1,
            grid=(parts, channels // TILE),
            in_specs=[
                pl.BlockSpec((1, times, TILE, signals), lambda s, c, _: (s, 0, c, 0)),
                pl.BlockSpec((TILE * TILE, TILE * TILE), lambda s, c, _: (0, 0)),
                pl.BlockSpec((1, signals), lambda s, c, _: (0, 0)),
            ],
            out_specs=[pl.BlockSpec(memory_space=pl.ANY)] * CHUNKS,
            scratch_shapes=[
                pltpu.VMEM((2, TILE, times, signals), jnp.bfloat16),
                pltpu.SemaphoreType.DMA((2, TILE)),
            ],
        ),
        out_shape=[shape] * CHUNKS,
        compiler_params=pltpu.CompilerParams(vmem_limit_bytes=40 * 2**20),
        cost_estimate=pl.CostEstimate(
            flops=2 * TILE * TILE * voltages.size, bytes_accessed=4 * voltages.size, transcendentals=0
        ),
        name="arrange",
    )(place, voltages, turn, keep)


def invert_factor(gram):
    count, rank = gram.shape[0], gram.shape[1]
    row_no = lax.broadcasted_iota(jnp.int32, (count, rank, rank), 1)
    col_no = lax.broadcasted_iota(jnp.int32, (count, rank, rank), 2)
    inverse = jnp.where(row_no == col_no, 1.0, 0.0)
    for j in range(rank):
        scale = 1.0 / jnp.sqrt(gram[:, j : j + 1, j : j + 1])
        under = jnp.where(row_no > j, gram[:, :, j : j + 1] * scale, 0.0)
        upper_row = gram[:, j : j + 1, :] * scale
        inverse_row = inverse[:, j : j + 1, :] * scale
        gram = gram - under * upper_row
        inverse = jnp.where(row_no == j, inverse_row, inverse - under * inverse_row)
    return inverse


def beam_kernel(freq_ref, x_ref, state_ref, delay_ref, out_ref, track_ref, image, gram, weight, clean):
    block, parts = x_ref.shape[1], x_ref.shape[2]
    signals = x_ref.shape[-1]
    beams, stations = delay_ref.shape
    owners, beam_rows = out_ref.shape[0], out_ref.shape[3]
    highest = lax.Precision.HIGHEST
    base = pl.program_id(0) * block

    def samples(i, part):
        return x_ref[:, i, part].reshape(-1, signals)

    track_ref[...] = state_ref[...]
    for part in range(parts):
        for i in range(block):
            x = samples(i, part)
            state = track_ref[i]
            y = lax.dot_general(
                state.astype(jnp.bfloat16), x, NT, preferred_element_type=jnp.float32
            ).astype(jnp.bfloat16)
            z = jnp.dot(y, x, preferred_element_type=jnp.float32) + x.shape[0] * state
            image[i] = z
            gram[i] = lax.dot_general(
                z, z, NT, precision=highest, preferred_element_type=jnp.float32
            )
        inverse = invert_factor(gram[...])
        for i in range(block):
            x = samples(i, part)
            state = jnp.dot(
                inverse[i], image[i], precision=highest, preferred_element_type=jnp.float32
            )
            track_ref[i] = state
            rows = state.astype(jnp.bfloat16)
            p = lax.dot_general(rows, x, NT, preferred_element_type=jnp.float32)
            lost = lax.dot_general(
                p.astype(jnp.bfloat16), rows, TN, preferred_element_type=jnp.float32
            )
            times = x.shape[0]
            clean[i, part * times : (part + 1) * times, :] = (
                x.astype(jnp.float32) - lost
            ).astype(jnp.bfloat16)

    factor = 1.0 / math.sqrt(stations)

    def form(i, carry):
        turns = delay_ref[...] * freq_ref[base + i]
        turns = turns - jnp.round(turns)
        square = turns * turns
        re = evaluate(COS, square, factor).astype(jnp.bfloat16)
        im = evaluate(SIN, square, factor) * turns
        weight[:beams, :stations] = re
        weight[:beams, stations:] = (-im).astype(jnp.bfloat16)
        weight[beams:, :stations] = im.astype(jnp.bfloat16)
        weight[beams:, stations:] = re
        formed = lax.dot_general(
            weight[...], clean[i], NT, preferred_element_type=jnp.float32
        ).astype(jnp.bfloat16)
        times = formed.shape[1] // parts
        for part in range(parts):
            out_ref[:, part, i] = formed[:, part * times : (part + 1) * times].reshape(
                owners, beam_rows, times
            )
        return carry

    lax.fori_loop(0, block, form, 0)


def form_beams(x, state, freq, delays, owners):
    sources, slots, parts, times, signals = x.shape
    rank = state.shape[1]
    beams, stations = delays.shape
    total = sources * times
    rows = 2 * beams // owners
    return pl.pallas_call(
        beam_kernel,
        grid=(slots // BLOCK,),
        in_specs=[
            pl.BlockSpec(memory_space=pltpu.SMEM),
            pl.BlockSpec((sources, BLOCK, parts, times, signals), lambda b: (0, b, 0, 0, 0)),
            pl.BlockSpec((BLOCK, rank, signals), lambda b: (b, 0, 0)),
            pl.BlockSpec((beams, stations), lambda b: (0, 0)),
        ],
        out_specs=[
            pl.BlockSpec((owners, parts, BLOCK, rows, total), lambda b: (0, 0, b, 0, 0)),
            pl.BlockSpec((BLOCK, rank, signals), lambda b: (b, 0, 0)),
        ],
        out_shape=[
            jax.ShapeDtypeStruct((owners, parts, slots, rows, total), jnp.bfloat16),
            jax.ShapeDtypeStruct(state.shape, jnp.float32),
        ],
        scratch_shapes=[
            pltpu.VMEM((BLOCK, rank, signals), jnp.float32),
            pltpu.VMEM((BLOCK, rank, rank), jnp.float32),
            pltpu.VMEM((2 * beams, 2 * stations), jnp.bfloat16),
            pltpu.VMEM((BLOCK, parts * total, signals), jnp.bfloat16),
        ],
        compiler_params=pltpu.CompilerParams(vmem_limit_bytes=48 * 2**20),
        cost_estimate=pl.CostEstimate(
            flops=slots * parts * 2 * total * signals * (2 * beams + 6 * rank) * 4,
            bytes_accessed=2 * x.size + 8 * state.size + 4 * slots * parts * beams * total,
            transcendentals=0,
        ),
        name="form_beams",
    )(freq, x, state, delays)


def per_device_blocks(voltages, subspace, order, beam_seeds, flagged, owners, groups):
    signals = voltages.shape[-1]
    stations = signals // 2
    slots = subspace.shape[1]
    per_group = order.shape[0]
    per = slots // CHUNKS
    marks = jnp.any(flagged[:, None] == jnp.arange(stations, dtype=jnp.int32)[None, :], axis=0)
    keep = jnp.where(marks, 0.0, 1.0).astype(jnp.float32)
    keep = jnp.concatenate([keep, keep])[None, :]
    slot_no = jnp.arange(per_group, dtype=jnp.int32)
    match = order[None, :] == slot_no[:, None]
    place = jnp.sum(jnp.where(match, slot_no[None, :], 0), axis=1).astype(jnp.int32)
    pieces = arrange(voltages, place, keep, owners, slots)

    group = lax.axis_index("chan")
    chosen = lax.dynamic_slice_in_dim(order, lax.axis_index("tm") * slots, slots)
    freq = 1.0 + (group * per_group + chosen).astype(jnp.float32) / CH
    station_no = jnp.arange(stations, dtype=jnp.int32) + 1
    delays = (beam_seeds[:, None] * station_no[None, :] % 65521).astype(jnp.float32) / 65521.0

    formed_all, tracked = [], []
    for chunk in range(CHUNKS):
        x = lax.all_to_all(pieces[chunk], "tm", split_axis=0, concat_axis=0, tiled=True)
        first = chunk * per
        formed, state = form_beams(
            x, subspace[0, first : first + per], freq[first : first + per], delays, groups
        )
        tracked.append(state)
        formed_all.append(lax.all_to_all(formed, "chan", split_axis=0, concat_axis=0, tiled=True))
    beams = jnp.concatenate(formed_all, axis=2)
    return jnp.swapaxes(beams, 0, 1), jnp.concatenate(tracked)[None]


def beam_weights(beam_seeds, channels, stations, total_channels):
    station_no = jnp.arange(stations, dtype=jnp.int32) + 1
    delays = (station_no[:, None] * beam_seeds[None, :] % 65521).astype(jnp.float32) / 65521.0
    frequency = 1.0 + channels.astype(jnp.float32) / total_channels
    angles = delays[None, :, :] * (TWO_PI * frequency)[:, None, None]
    factor = 1.0 / math.sqrt(stations)
    cosine = jnp.cos(angles) * factor
    sine_part = jnp.sin(angles) * factor
    upper = jnp.concatenate([cosine, sine_part], axis=2)
    under = jnp.concatenate([-sine_part, cosine], axis=2)
    return jnp.concatenate([upper, under], axis=1).astype(jnp.bfloat16)


def power_step(voltage_input, tracked, steering_weight):
    sample_count = voltage_input.shape[0]
    coarse_channel = tracked.astype(jnp.bfloat16)
    projected_input = jnp.einsum(
        "xbj,bqj->bxq", voltage_input, coarse_channel, preferred_element_type=jnp.float32
    ).astype(jnp.bfloat16)
    beam_image = (
        jnp.einsum(
            "nwg,wny->ngy", projected_input, voltage_input, preferred_element_type=jnp.float32
        )
        + sample_count * tracked
    )
    gram = jnp.einsum("crs,cks->crk", beam_image, beam_image, precision=lax.Precision.HIGHEST)
    lower = jnp.linalg.cholesky(gram)
    tracked = jax.scipy.linalg.solve_triangular(lower, beam_image, lower=True)
    subspace_vectors = tracked.astype(jnp.bfloat16)
    lengthwise_axis = jnp.einsum(
        "xbj,bqj->bxq", voltage_input, subspace_vectors, preferred_element_type=jnp.float32
    ).astype(jnp.bfloat16)
    mixing = jnp.einsum(
        "crs,csb->crb", subspace_vectors, steering_weight, preferred_element_type=jnp.float32
    ).astype(jnp.bfloat16)
    direct_output = jnp.einsum(
        "edi,diy->dye", voltage_input, steering_weight, preferred_element_type=jnp.float32
    )
    beams = direct_output - jnp.einsum(
        "ctr,crb->cbt", lengthwise_axis, mixing, preferred_element_type=jnp.float32
    )
    return (tracked, beams.astype(jnp.bfloat16))


def per_device_plain(voltages, subspace, order, beam_seeds, flagged):
    signals = voltages.shape[-1]
    stations = signals // 2
    slots = subspace.shape[1]
    per_group = order.shape[0]
    marks = jnp.any(flagged[:, None] == jnp.arange(stations, dtype=jnp.int32)[None, :], axis=0)
    keep = jnp.where(marks, 0.0, 1.0).astype(jnp.bfloat16)
    keep = jnp.concatenate([keep, keep])
    ordered = jnp.take(voltages, order, axis=2) * keep
    group = lax.axis_index("chan")
    first_slot = lax.axis_index("tm") * slots
    chosen = lax.dynamic_slice_in_dim(order, first_slot, slots)
    channels = group * per_group + chosen
    steering_weight = beam_weights(beam_seeds, channels, stations, CH)
    state = subspace[0]
    results = []
    for part in range(voltages.shape[0]):
        turned = lax.all_to_all(ordered[part], "tm", split_axis=1, concat_axis=0, tiled=True)
        state, formed = power_step(turned, state, steering_weight)
        results.append(
            lax.all_to_all(formed[None], "chan", split_axis=2, concat_axis=0, tiled=True)
        )
    output = jnp.stack(results)
    return (output, state[None])


def solution(mesh):
    owners, groups = mesh.shape["tm"], mesh.shape["chan"]

    def per_device(voltages, subspace, order, beam_seeds, flagged):
        times, channels = voltages.shape[1], voltages.shape[2]
        whole = (
            times % TILE == 0
            and channels % TILE == 0
            and subspace.shape[1] % (CHUNKS * BLOCK) == 0
            and 2 * beam_seeds.shape[0] % (groups * TILE) == 0
        )
        if whole:
            return per_device_blocks(
                voltages, subspace, order, beam_seeds, flagged, owners, groups
            )
        return per_device_plain(voltages, subspace, order, beam_seeds, flagged)

    return jax.shard_map(
        per_device,
        mesh=mesh,
        in_specs=(P(None, "tm", "chan", None), P("chan", "tm", None, None), P(), P(), P()),
        out_specs=(P(None, None, "tm", "chan", None), P("chan", "tm", None, None)),
        check_vma=False,
    )
```

```python
import functools
import math

import jax
import jax.numpy as jnp
import numpy as np
from jax import lax
from jax.experimental import pallas as pl
from jax.experimental.pallas import tpu as pltpu
from jax.sharding import PartitionSpec as P

CH = 2048
CHUNKS = 8
BLOCK = 8
TILE = 16

TWO_PI = 2.0 * math.pi
NT = (((1,), (1,)), ((), ()))
TN = (((0,), (0,)), ((), ()))


def series(func, odd):
    fit = np.polynomial.chebyshev.Chebyshev.interpolate(
        lambda r: func(TWO_PI * r), 11 if odd else 10, domain=[-0.5, 0.5]
    )
    powers = fit.convert(kind=np.polynomial.Polynomial).coef
    return [float(value) for value in powers[1 if odd else 0 :: 2]]


COS = series(np.cos, False)
SIN = series(np.sin, True)


def evaluate(coefficients, square, factor):
    total = coefficients[-1] * factor
    for value in coefficients[-2::-1]:
        total = total * square + value * factor
    return total


def arrange_kernel(chunks, per, place_ref, volt_ref, turn_ref, keep_ref, *rest):
    outs, (held, sems) = rest[:chunks], rest[chunks:]
    part, block = pl.program_id(0), pl.program_id(1)
    blocks = pl.num_programs(1)
    step = part * blocks + block
    half = lax.rem(step, 2)
    times = volt_ref.shape[1]

    def drain(which):
        for row in range(TILE):
            pltpu.make_async_copy(
                held.at[which, row], outs[0].at[0, 0, 0], sems.at[which, row]
            ).wait()

    @pl.when(step >= 2)
    def _():
        drain(half)

    for start in range(0, times, TILE):
        rows = volt_ref[0, start : start + TILE].reshape(TILE * TILE, -1)
        turned = jnp.dot(turn_ref[...], rows, preferred_element_type=jnp.float32)
        turned = (turned * keep_ref[...]).astype(jnp.bfloat16)
        held[half, :, start : start + TILE, :] = turned.reshape(TILE, TILE, -1)
    for row in range(TILE):
        place = place_ref[block * TILE + row]
        slots = chunks * per
        owner, local = place // slots, lax.rem(place, slots)
        chunk, inner = local // per, lax.rem(local, per)
        for index in range(chunks):

            @pl.when(chunk == index)
            def _():
                pltpu.make_async_copy(
                    held.at[half, row], outs[index].at[owner, inner, part], sems.at[half, row]
                ).start()

    @pl.when(step == 2 * blocks - 1)
    def _():
        drain(1 - half)
        drain(half)


def arrange(voltages, place, keep, owners, slots):
    parts, times, channels, signals = voltages.shape
    per = slots // CHUNKS
    row = jnp.arange(TILE * TILE)
    turn = (row[None, :] == (row % TILE * TILE + row // TILE)[:, None]).astype(jnp.bfloat16)
    shape = jax.ShapeDtypeStruct((owners, per, parts, times, signals), jnp.bfloat16)
    return pl.pallas_call(
        functools.partial(arrange_kernel, CHUNKS, per),
        grid_spec=pltpu.PrefetchScalarGridSpec(
            num_scalar_prefetch=1,
            grid=(parts, channels // TILE),
            in_specs=[
                pl.BlockSpec((1, times, TILE, signals), lambda s, c, _: (s, 0, c, 0)),
                pl.BlockSpec((TILE * TILE, TILE * TILE), lambda s, c, _: (0, 0)),
                pl.BlockSpec((1, signals), lambda s, c, _: (0, 0)),
            ],
            out_specs=[pl.BlockSpec(memory_space=pl.ANY)] * CHUNKS,
            scratch_shapes=[
                pltpu.VMEM((2, TILE, times, signals), jnp.bfloat16),
                pltpu.SemaphoreType.DMA((2, TILE)),
            ],
        ),
        out_shape=[shape] * CHUNKS,
        compiler_params=pltpu.CompilerParams(vmem_limit_bytes=40 * 2**20),
        cost_estimate=pl.CostEstimate(
            flops=2 * TILE * TILE * voltages.size, bytes_accessed=4 * voltages.size, transcendentals=0
        ),
        name="arrange",
    )(place, voltages, turn, keep)


def invert_factor(gram):
    count, rank = gram.shape[0], gram.shape[1]
    row_no = lax.broadcasted_iota(jnp.int32, (count, rank, rank), 1)
    col_no = lax.broadcasted_iota(jnp.int32, (count, rank, rank), 2)
    inverse = jnp.where(row_no == col_no, 1.0, 0.0)
    for j in range(rank):
        scale = 1.0 / jnp.sqrt(gram[:, j : j + 1, j : j + 1])
        under = jnp.where(row_no > j, gram[:, :, j : j + 1] * scale, 0.0)
        upper_row = gram[:, j : j + 1, :] * scale
        inverse_row = inverse[:, j : j + 1, :] * scale
        gram = gram - under * upper_row
        inverse = jnp.where(row_no == j, inverse_row, inverse - under * inverse_row)
    return inverse


def beam_kernel(count, freq_ref, source_ref, *rest):
    arrived, rest = rest[:count], rest[count:]
    state_ref, delay_ref, out_ref, track_ref, image, gram, weight, clean, x_ref = rest
    block, parts = x_ref.shape[1], x_ref.shape[2]
    signals = x_ref.shape[-1]
    for index in range(count):
        x_ref[source_ref[index]] = arrived[index][...]
    beams, stations = delay_ref.shape
    owners, beam_rows = out_ref.shape[0], out_ref.shape[3]
    highest = lax.Precision.HIGHEST
    base = pl.program_id(0) * block

    def samples(i, part):
        return x_ref[:, i, part].reshape(-1, signals)

    track_ref[...] = state_ref[...]
    for part in range(parts):
        for i in range(block):
            x = samples(i, part)
            state = track_ref[i]
            y = lax.dot_general(
                state.astype(jnp.bfloat16), x, NT, preferred_element_type=jnp.float32
            ).astype(jnp.bfloat16)
            z = jnp.dot(y, x, preferred_element_type=jnp.float32) + x.shape[0] * state
            image[i] = z
            gram[i] = lax.dot_general(
                z, z, NT, precision=highest, preferred_element_type=jnp.float32
            )
        inverse = invert_factor(gram[...])
        for i in range(block):
            x = samples(i, part)
            state = jnp.dot(
                inverse[i], image[i], precision=highest, preferred_element_type=jnp.float32
            )
            track_ref[i] = state
            rows = state.astype(jnp.bfloat16)
            p = lax.dot_general(rows, x, NT, preferred_element_type=jnp.float32)
            lost = lax.dot_general(
                p.astype(jnp.bfloat16), rows, TN, preferred_element_type=jnp.float32
            )
            times = x.shape[0]
            clean[i, part * times : (part + 1) * times, :] = (
                x.astype(jnp.float32) - lost
            ).astype(jnp.bfloat16)

    factor = 1.0 / math.sqrt(stations)

    def form(i, carry):
        turns = delay_ref[...] * freq_ref[base + i]
        turns = turns - jnp.round(turns)
        square = turns * turns
        re = evaluate(COS, square, factor).astype(jnp.bfloat16)
        im = evaluate(SIN, square, factor) * turns
        weight[:beams, :stations] = re
        weight[:beams, stations:] = (-im).astype(jnp.bfloat16)
        weight[beams:, :stations] = im.astype(jnp.bfloat16)
        weight[beams:, stations:] = re
        formed = lax.dot_general(
            weight[...], clean[i], NT, preferred_element_type=jnp.float32
        ).astype(jnp.bfloat16)
        times = formed.shape[1] // parts
        for part in range(parts):
            out_ref[:, part, i] = formed[:, part * times : (part + 1) * times].reshape(
                owners, beam_rows, times
            )
        return carry

    lax.fori_loop(0, block, form, 0)


def form_beams(pieces, source_no, state, freq, delays, owners):
    sources = len(pieces)
    slots, parts, times, signals = pieces[0].shape
    rank = state.shape[1]
    beams, stations = delays.shape
    total = sources * times
    rows = 2 * beams // owners
    return pl.pallas_call(
        functools.partial(beam_kernel, sources),
        grid=(slots // BLOCK,),
        in_specs=[
            pl.BlockSpec(memory_space=pltpu.SMEM),
            pl.BlockSpec(memory_space=pltpu.SMEM),
            *[pl.BlockSpec((BLOCK, parts, times, signals), lambda b: (b, 0, 0, 0))] * sources,
            pl.BlockSpec((BLOCK, rank, signals), lambda b: (b, 0, 0)),
            pl.BlockSpec((beams, stations), lambda b: (0, 0)),
        ],
        out_specs=[
            pl.BlockSpec((owners, parts, BLOCK, rows, total), lambda b: (0, 0, b, 0, 0)),
            pl.BlockSpec((BLOCK, rank, signals), lambda b: (b, 0, 0)),
        ],
        out_shape=[
            jax.ShapeDtypeStruct((owners, parts, slots, rows, total), jnp.bfloat16),
            jax.ShapeDtypeStruct(state.shape, jnp.float32),
        ],
        scratch_shapes=[
            pltpu.VMEM((BLOCK, rank, signals), jnp.float32),
            pltpu.VMEM((BLOCK, rank, rank), jnp.float32),
            pltpu.VMEM((2 * beams, 2 * stations), jnp.bfloat16),
            pltpu.VMEM((BLOCK, parts * total, signals), jnp.bfloat16),
            pltpu.VMEM((sources, BLOCK, parts, times, signals), jnp.bfloat16),
        ],
        compiler_params=pltpu.CompilerParams(vmem_limit_bytes=48 * 2**20),
        cost_estimate=pl.CostEstimate(
            flops=slots * parts * 2 * total * signals * (2 * beams + 6 * rank) * 4,
            bytes_accessed=2 * sources * pieces[0].size + 8 * state.size + 4 * slots * parts * beams * total,
            transcendentals=0,
        ),
        name="form_beams",
    )(freq, source_no, *pieces, state, delays)


def per_device_blocks(voltages, subspace, order, beam_seeds, flagged, owners, groups):
    signals = voltages.shape[-1]
    stations = signals // 2
    slots = subspace.shape[1]
    per_group = order.shape[0]
    per = slots // CHUNKS
    marks = jnp.any(flagged[:, None] == jnp.arange(stations, dtype=jnp.int32)[None, :], axis=0)
    keep = jnp.where(marks, 0.0, 1.0).astype(jnp.float32)
    keep = jnp.concatenate([keep, keep])[None, :]
    slot_no = jnp.arange(per_group, dtype=jnp.int32)
    match = order[None, :] == slot_no[:, None]
    place = jnp.sum(jnp.where(match, slot_no[None, :], 0), axis=1).astype(jnp.int32)
    pieces = arrange(voltages, place, keep, owners, slots)

    group = lax.axis_index("chan")
    chosen = lax.dynamic_slice_in_dim(order, lax.axis_index("tm") * slots, slots)
    freq = 1.0 + (group * per_group + chosen).astype(jnp.float32) / CH
    station_no = jnp.arange(stations, dtype=jnp.int32) + 1
    delays = (beam_seeds[:, None] * station_no[None, :] % 65521).astype(jnp.float32) / 65521.0

    me = lax.axis_index("tm")
    source_no = jnp.bitwise_xor(me, jnp.arange(owners, dtype=jnp.int32)).astype(jnp.int32)
    formed_all, tracked, arrived = [], [], None

    def form_chunk(chunk, arrived):
        first = chunk * per
        formed, state = form_beams(
            arrived,
            source_no,
            subspace[0, first : first + per],
            freq[first : first + per],
            delays,
            groups,
        )
        tracked.append(state)
        formed_all.append(lax.all_to_all(formed, "chan", split_axis=0, concat_axis=0, tiled=True))

    for chunk in range(CHUNKS):
        sent = [
            lax.dynamic_index_in_dim(pieces[chunk], source_no[j], 0, keepdims=False)
            for j in range(owners)
        ]
        if arrived is not None:
            sent, arrived = lax.optimization_barrier((sent, arrived))
            form_chunk(chunk - 1, arrived)
        arrived = [sent[0]] + [
            lax.ppermute(sent[j], "tm", [(i, i ^ j) for i in range(owners)])
            for j in range(1, owners)
        ]
    form_chunk(CHUNKS - 1, arrived)
    beams = jnp.concatenate(formed_all, axis=2)
    return jnp.swapaxes(beams, 0, 1), jnp.concatenate(tracked)[None]


def beam_weights(beam_seeds, channels, stations, total_channels):
    station_no = jnp.arange(stations, dtype=jnp.int32) + 1
    delays = (station_no[:, None] * beam_seeds[None, :] % 65521).astype(jnp.float32) / 65521.0
    frequency = 1.0 + channels.astype(jnp.float32) / total_channels
    angles = delays[None, :, :] * (TWO_PI * frequency)[:, None, None]
    factor = 1.0 / math.sqrt(stations)
    cosine = jnp.cos(angles) * factor
    sine_part = jnp.sin(angles) * factor
    upper = jnp.concatenate([cosine, sine_part], axis=2)
    under = jnp.concatenate([-sine_part, cosine], axis=2)
    return jnp.concatenate([upper, under], axis=1).astype(jnp.bfloat16)


def power_step(voltage_input, tracked, steering_weight):
    sample_count = voltage_input.shape[0]
    coarse_channel = tracked.astype(jnp.bfloat16)
    projected_input = jnp.einsum(
        "xbj,bqj->bxq", voltage_input, coarse_channel, preferred_element_type=jnp.float32
    ).astype(jnp.bfloat16)
    beam_image = (
        jnp.einsum(
            "nwg,wny->ngy", projected_input, voltage_input, preferred_element_type=jnp.float32
        )
        + sample_count * tracked
    )
    gram = jnp.einsum("crs,cks->crk", beam_image, beam_image, precision=lax.Precision.HIGHEST)
    lower = jnp.linalg.cholesky(gram)
    tracked = jax.scipy.linalg.solve_triangular(lower, beam_image, lower=True)
    subspace_vectors = tracked.astype(jnp.bfloat16)
    lengthwise_axis = jnp.einsum(
        "xbj,bqj->bxq", voltage_input, subspace_vectors, preferred_element_type=jnp.float32
    ).astype(jnp.bfloat16)
    mixing = jnp.einsum(
        "crs,csb->crb", subspace_vectors, steering_weight, preferred_element_type=jnp.float32
    ).astype(jnp.bfloat16)
    direct_output = jnp.einsum(
        "edi,diy->dye", voltage_input, steering_weight, preferred_element_type=jnp.float32
    )
    beams = direct_output - jnp.einsum(
        "ctr,crb->cbt", lengthwise_axis, mixing, preferred_element_type=jnp.float32
    )
    return (tracked, beams.astype(jnp.bfloat16))


def per_device_plain(voltages, subspace, order, beam_seeds, flagged):
    signals = voltages.shape[-1]
    stations = signals // 2
    slots = subspace.shape[1]
    per_group = order.shape[0]
    marks = jnp.any(flagged[:, None] == jnp.arange(stations, dtype=jnp.int32)[None, :], axis=0)
    keep = jnp.where(marks, 0.0, 1.0).astype(jnp.bfloat16)
    keep = jnp.concatenate([keep, keep])
    ordered = jnp.take(voltages, order, axis=2) * keep
    group = lax.axis_index("chan")
    first_slot = lax.axis_index("tm") * slots
    chosen = lax.dynamic_slice_in_dim(order, first_slot, slots)
    channels = group * per_group + chosen
    steering_weight = beam_weights(beam_seeds, channels, stations, CH)
    state = subspace[0]
    results = []
    for part in range(voltages.shape[0]):
        turned = lax.all_to_all(ordered[part], "tm", split_axis=1, concat_axis=0, tiled=True)
        state, formed = power_step(turned, state, steering_weight)
        results.append(
            lax.all_to_all(formed[None], "chan", split_axis=2, concat_axis=0, tiled=True)
        )
    output = jnp.stack(results)
    return (output, state[None])


def solution(mesh):
    owners, groups = mesh.shape["tm"], mesh.shape["chan"]

    def per_device(voltages, subspace, order, beam_seeds, flagged):
        times, channels = voltages.shape[1], voltages.shape[2]
        whole = (
            owners & (owners - 1) == 0
            and times % TILE == 0
            and channels % TILE == 0
            and subspace.shape[1] % (CHUNKS * BLOCK) == 0
            and 2 * beam_seeds.shape[0] % (groups * TILE) == 0
        )
        if whole:
            return per_device_blocks(
                voltages, subspace, order, beam_seeds, flagged, owners, groups
            )
        return per_device_plain(voltages, subspace, order, beam_seeds, flagged)

    return jax.shard_map(
        per_device,
        mesh=mesh,
        in_specs=(P(None, "tm", "chan", None), P("chan", "tm", None, None), P(), P(), P()),
        out_specs=(P(None, None, "tm", "chan", None), P("chan", "tm", None, None)),
        check_vma=False,
    )
```
